1024 devices in a mesh: rep: 32 (over x, y, core), fsdp: 32 (over z).
Axes of the slice: x: 4, y: 4, z: 32, core: 2. Of those that a mesh axis runs over, the one named last changes fastest.
Arguments:
- partials: bfloat16 [32, 64, 512, 512], P('rep', None, 'fsdp'), may hold values from -2.6 to 2.6
- owner: int32 [64], P('rep'), may hold values from 0 to 31, as said below
- left_stats: bfloat16 [64, 512, 512], P('rep', 'fsdp'), may hold values from -1.2 to 9.2, as said below
- right_stats: bfloat16 [64, 512, 512], P('rep', 'fsdp'), may hold values from -1.2 to 9.2, as said below
- left_root: bfloat16 [64, 512, 512], P('rep', 'fsdp'), may hold values from -0.6 to 4.6, as said below
- right_root: bfloat16 [64, 512, 512], P('rep', 'fsdp'), may hold values from -0.6 to 4.6, as said below
Outputs:
- update: bfloat16 [64, 512, 512], P('rep', 'fsdp')
- new_left: bfloat16 [64, 512, 512], P('rep', 'fsdp')
- new_right: bfloat16 [64, 512, 512], P('rep', 'fsdp')
The draws below stay inside these ranges and needn't reach their ends.
Inputs may be any that keep to these rules, and one draw needn't show every extreme that they name: Within each group of 2 blocks (block b is in group b // 2) at most 2 blocks share an owner, and in some group of every draw 2 do. `left_stats`: symmetric blocks. `right_stats`: symmetric blocks. `left_root`: symmetric blocks. `right_root`: symmetric blocks.
All inputs are finite; a program needn't handle non-finite values.
Results may differ from the reference program's by a relative error of at most 0.023.
Values may be sent and summed in bfloat16 or wider, within the bound.
No kernel may reach another device: no remote copies, remote signals or barrier semaphores. Data moves between devices by JAX's collectives and lax.ppermute only.
A program may use at most 32 MiB of HBM per device.

```python
import jax
import jax.numpy as jnp
from jax import lax

BLK = 512
GRP = 2
NBLK = 64
N_REP = 32
N_FSDP = 32


def symmetric_blocks(key, count, order, lowest, highest, spread):
    first_key, second_key = jax.random.split(key)
    diagonal = jnp.exp(jax.random.uniform(first_key, (count, order), jnp.float32, jnp.log(lowest), jnp.log(highest)))
    noise = jnp.clip(jax.random.normal(second_key, (count, order, order), jnp.float32), -4.0, 4.0)
    offdiag = spread * 0.7071 * (noise + jnp.swapaxes(noise, 1, 2))
    eye_mask = lax.broadcasted_iota(jnp.int32, (order, order), 0) == lax.broadcasted_iota(jnp.int32, (order, order), 1)
    return jnp.where(eye_mask[None], diagonal[:, :, None], offdiag)


def draw_left_stats(key, part):
    key = jax.random.fold_in(key, 23)
    return symmetric_blocks(key, NBLK, BLK, 0.5, 4.0, 0.05).astype(jnp.bfloat16)


def draw_right_stats(key, part):
    key = jax.random.fold_in(key, 24)
    return symmetric_blocks(key, NBLK, BLK, 0.5, 4.0, 0.05).astype(jnp.bfloat16)


def draw_left_root(key, part):
    key = jax.random.fold_in(key, 21)
    return symmetric_blocks(key, NBLK, BLK, 0.5, 2.0, 0.03).astype(jnp.bfloat16)


def draw_right_root(key, part):
    key = jax.random.fold_in(key, 22)
    return symmetric_blocks(key, NBLK, BLK, 0.5, 2.0, 0.03).astype(jnp.bfloat16)


def draw_partials(key, part):
    key = jax.random.fold_in(key, 25)
    keys = jax.random.split(key, 3)
    row_scale = jnp.exp(jax.random.uniform(keys[0], (1, NBLK, BLK, 1), jnp.float32, 0.0, 1.1513))
    col_scale = jnp.exp(jax.random.uniform(keys[1], (1, NBLK, 1, BLK), jnp.float32, 0.0, 1.1513))
    noise = jnp.clip(jax.random.normal(keys[2], (N_REP, NBLK, BLK, BLK), jnp.float32), -5.0, 5.0)
    return (0.05 * row_scale * col_scale * noise).astype(jnp.bfloat16)


def draw_owner(key, part):
    key = jax.random.fold_in(key, 26)
    keys = jax.random.split(key, 4)
    first = jax.random.randint(keys[0], (N_REP,), 0, N_FSDP)
    offset = jax.random.randint(keys[1], (N_REP,), 1, N_FSDP)
    coins = jax.random.randint(keys[2], (N_REP,), 0, 2)
    forced = jax.random.randint(keys[3], (), 0, N_REP)
    coins = jnp.where(jnp.arange(N_REP) == forced, 1, coins)
    second = jnp.where(coins == 1, first, (first + offset) % N_FSDP)
    return jnp.stack([first, second], axis=1).reshape(NBLK).astype(jnp.int32)


def setup_inputs(seed: int = 0) -> dict:
    key_list = jax.random.split(jax.random.key(seed), 7)
    return {
        "partials": draw_partials(jax.random.fold_in(key_list[6], 71), 0),
        "owner": draw_owner(jax.random.fold_in(key_list[6], 71), 0),
        "left_stats": draw_left_stats(jax.random.fold_in(key_list[6], 71), 0),
        "right_stats": draw_right_stats(jax.random.fold_in(key_list[6], 71), 0),
        "left_root": draw_left_root(jax.random.fold_in(key_list[6], 71), 0),
        "right_root": draw_right_root(jax.random.fold_in(key_list[6], 71), 0),
    }


BETA = 0.9
EPS = 1e-06

def graft_block(grad, left_inv, right_inv):
    first = jnp.dot(left_inv, grad, preferred_element_type=jnp.float32).astype(jnp.bfloat16)
    second = jnp.dot(first, right_inv, preferred_element_type=jnp.float32)
    grad_wide = grad.astype(jnp.float32)
    factor = jnp.sqrt(jnp.mean(grad_wide * grad_wide) + EPS) / jnp.sqrt(jnp.mean(second * second) + EPS)
    return (second * factor).astype(jnp.bfloat16)

def reference(partials, owner, left_stats, right_stats, left_root, right_root):

    def add_replica(index, total):
        return total + partials[index].astype(jnp.float32)
    total = lax.fori_loop(0, N_REP, add_replica, jnp.zeros((NBLK, BLK, BLK), jnp.float32))
    grad = total.astype(jnp.bfloat16)
    owners = owner.reshape(N_REP, GRP)
    sharing = owners[:, :, None] == owners[:, None, :]
    lower = owners[:, None, :] < owners[:, :, None]
    earlier = jnp.arange(GRP)[None, :] < jnp.arange(GRP)[:, None]
    position = lax.optimization_barrier(jnp.sum((lower | sharing & earlier[None]).astype(jnp.int32), axis=2))
    slot_index = jnp.arange(N_REP, dtype=jnp.int32)[:, None] * GRP + position
    slot_index = slot_index.reshape(NBLK).astype(jnp.int32)

    def one_block(items):
        block, left_old, right_old, where = items
        left_gram = jnp.dot(block, block.T, preferred_element_type=jnp.float32)
        right_gram = jnp.dot(block.T, block, preferred_element_type=jnp.float32)
        left_next = (BETA * left_old.astype(jnp.float32) + (1.0 - BETA) / BLK * left_gram).astype(jnp.bfloat16)
        right_next = (BETA * right_old.astype(jnp.float32) + (1.0 - BETA) / BLK * right_gram).astype(jnp.bfloat16)
        left_inv = lax.dynamic_index_in_dim(left_root, where, 0, keepdims=False)
        right_inv = lax.dynamic_index_in_dim(right_root, where, 0, keepdims=False)
        return (graft_block(block, left_inv, right_inv), left_next, right_next)
    update, new_left, new_right = lax.map(one_block, (grad, left_stats, right_stats, slot_index))
    return (update, new_left, new_right)
```

```python
import jax
import jax.numpy as jnp
from jax import lax
from jax.sharding import Mesh, PartitionSpec as P

BETA = 0.9
EPS = 1e-06
NARROW = jnp.bfloat16
WIDE = jnp.float32


def split_terms(value):
    high = value.astype(NARROW)
    rest = value - high.astype(WIDE)
    mid = rest.astype(NARROW)
    low = (rest - mid.astype(WIDE)).astype(NARROW)
    return [high, mid, low]


def mm(a, b, dims, out=WIDE):
    return lax.dot_general(a, b, (dims, ((), ())), preferred_element_type=WIDE).astype(out)


def block_rows(rows_g, rows_l, gathered_g, gathered_r, my_row, n_planes, n_rows):
    order = gathered_g.shape[0]
    natural = lax.broadcasted_iota(jnp.int32, (order, order), 0)
    stored = lax.broadcasted_iota(jnp.int32, (order, order), 1)
    shuffle = (natural == (stored % n_planes) * n_rows + stored // n_planes).astype(NARROW)
    pick = (
        lax.broadcasted_iota(jnp.int32, (order, n_planes), 0)
        == lax.broadcasted_iota(jnp.int32, (order, n_planes), 1) * n_rows + my_row
    ).astype(NARROW)
    across = ((1,), (0,))
    first = mm(mm(rows_l, shuffle, across, NARROW), gathered_g, across, NARROW)
    second = mm(mm(first, shuffle, across, NARROW), gathered_r, across)
    left_gram = mm(mm(rows_g, gathered_g, ((1,), (1,)), NARROW), shuffle, ((1,), (1,)), NARROW)
    columns = mm(gathered_g, pick, across, NARROW)
    right_gram = mm(columns, gathered_g, ((0,), (0,)), NARROW)
    wide_g = rows_g.astype(WIDE)
    terms = split_terms(jnp.sum(second * second)) + split_terms(jnp.sum(wide_g * wide_g))
    lane = lax.broadcasted_iota(jnp.int32, (n_planes, order), 1)
    scalars = jnp.zeros((n_planes, order), NARROW)
    for number, term in enumerate(terms):
        scalars = jnp.where(lane == number, term, scalars)
    return second.astype(NARROW), left_gram, right_gram, scalars


def local(partials, owner, left_stats, right_stats, left_root, right_root):
    n_xy = lax.axis_size("x") * lax.axis_size("y")
    n_z = lax.axis_size("z")
    core = lax.axis_index("c")
    my_row = lax.axis_index("x") * lax.axis_size("y") + lax.axis_index("y")
    _, n_blocks, n_rows, order = partials.shape
    groups = n_blocks // 2
    lanes = min(128, order)
    chunks = order // lanes

    swapped = owner[1] < owner[0]
    roots = jnp.stack([left_root, right_root], axis=0)
    roots = jnp.where(swapped, roots[:, ::-1], roots)

    blocks = partials[0].reshape(groups, 2, n_rows, order)
    keep = lax.dynamic_index_in_dim(blocks, core, 1, keepdims=False)
    send = lax.dynamic_index_in_dim(blocks, 1 - core, 1, keepdims=False)
    keep_roots = lax.dynamic_index_in_dim(roots, core, 1, keepdims=False)
    send_roots = lax.dynamic_index_in_dim(roots, 1 - core, 1, keepdims=False)
    swap = [(0, 1), (1, 0)]
    got = lax.ppermute(send, "c", swap)
    got_roots = lax.ppermute(send_roots, "c", swap)
    pair = (keep.astype(WIDE) + got.astype(WIDE)).astype(NARROW)
    zero_first = core == 0
    both_roots = jnp.stack(
        [jnp.where(zero_first, keep_roots, got_roots), jnp.where(zero_first, got_roots, keep_roots)], axis=0
    )

    outgoing = jnp.concatenate(
        [pair.transpose(1, 0, 2), both_roots.reshape(4, n_rows, order).transpose(1, 0, 2)], axis=1
    )
    arrived = lax.all_to_all(outgoing, ("x", "y"), 0, 0, tiled=True)
    grad = jnp.sum(arrived[:, :groups].astype(WIDE), axis=0).astype(NARROW)
    roots_here = arrived[:, groups:].reshape(groups, 2, order)

    to_planes = jnp.concatenate([grad[:, None], roots_here], axis=1).reshape(groups, 3 * chunks, lanes)
    in_plane = lax.all_to_all(to_planes, "z", 0, 0, tiled=True).reshape(n_z, 3, order)
    rows_g, rows_l, rows_r = in_plane[:, 0], in_plane[:, 1], in_plane[:, 2]

    copies = jnp.broadcast_to(jnp.concatenate([rows_g, rows_r], axis=0)[None], (n_xy, 2 * n_z, order))
    gathered = lax.all_to_all(copies, ("x", "y"), 0, 0, tiled=True)
    gathered_g = gathered[:, :n_z].reshape(order, order)
    gathered_r = gathered[:, n_z:].reshape(order, order)

    results = block_rows(rows_g, rows_l, gathered_g, gathered_r, my_row, n_z, n_rows)

    back = jnp.stack(results, axis=1).reshape(n_z, 4 * chunks, lanes)
    back = lax.all_to_all(back, "z", 0, 0, tiled=True)
    back = lax.all_to_all(back, ("x", "y", "c"), 0, 0, tiled=True)
    back = back.reshape(n_xy, 2, 4, order).transpose(2, 1, 0, 3).astype(WIDE)
    second, left_gram, right_gram, scalars = back[0], back[1], back[2], back[3]
    sums = jnp.sum(scalars, axis=1)
    second_sq = sums[:, 0] + sums[:, 1] + sums[:, 2]
    grad_sq = sums[:, 3] + sums[:, 4] + sums[:, 5]
    entries = order * order
    factor = jnp.sqrt(grad_sq / entries + EPS) / jnp.sqrt(second_sq / entries + EPS)
    update = (second * factor[:, None, None]).astype(NARROW)
    scale = (1.0 - BETA) / order
    new_left = (BETA * left_stats.astype(WIDE) + scale * left_gram).astype(NARROW)
    new_right = (BETA * right_stats.astype(WIDE) + scale * right_gram).astype(NARROW)
    return update, new_left, new_right


def solution(mesh, grid=(4, 4, 2)):
    n_z = mesh.devices.shape[1]
    fine = Mesh(mesh.devices.reshape(*grid, n_z), ("x", "y", "c", "z"))
    rep = ("x", "y", "c")
    rows = P(rep, "z", None)
    return jax.shard_map(
        local,
        mesh=fine,
        in_specs=(P(rep, None, "z", None), P(rep), rows, rows, rows, rows),
        out_specs=(rows, rows, rows),
        check_vma=False,
    )
```

```python
import jax
import jax.numpy as jnp
from jax import lax
from jax.sharding import Mesh, PartitionSpec as P

BETA = 0.9
EPS = 1e-06
NARROW = jnp.bfloat16
WIDE = jnp.float32
REP = ("x", "y", "c")
EVERY = ("x", "y", "c", "z")


def routes(n_rep, n_z):
    half = n_rep // 2
    pairs = []
    for g in range(n_rep):
        for z in range(n_z):
            q = (g + z) % n_rep
            pairs.append((g * n_z + z, (q % half * 2 + q // half) * n_z + g))
    return pairs


def mm(a, b, left, right, out=WIDE):
    dims = (((left,), (right,)), ((), ()))
    return lax.dot_general(a, b, dims, preferred_element_type=WIDE).astype(out)


def block_rows(grad, left, right, my_xy, plane, half, n_rows):
    order = grad.shape[0]
    mine = 2 * n_rows

    def place(stored):
        device = stored // n_rows
        slab = (device // 2 + half * (device % 2) + 2 * half - plane) % (2 * half)
        return slab * n_rows + stored % n_rows

    shuffle = (
        lax.broadcasted_iota(jnp.int32, (order, order), 1) == place(lax.broadcasted_iota(jnp.int32, (order, order), 0))
    ).astype(NARROW)
    pick = (
        lax.broadcasted_iota(jnp.int32, (order, mine), 0)
        == place(lax.broadcasted_iota(jnp.int32, (order, mine), 1) + my_xy * mine)
    ).astype(NARROW)
    first = mm(left, grad, 0, 0, NARROW)
    second = mm(first, right, 1, 1)
    wide = grad.astype(WIDE)
    entries = order * order
    factor = jnp.sqrt(jnp.sum(wide * wide) / entries + EPS) / jnp.sqrt(jnp.sum(second * second) / entries + EPS)
    first_mine = mm(pick, first, 0, 0, NARROW)
    update = (mm(first_mine, right, 1, 1) * factor).astype(NARROW)
    update = mm(update, shuffle, 1, 0, NARROW)
    grad_mine = lax.dynamic_slice_in_dim(grad, my_xy * mine, mine, 0)
    left_gram = mm(mm(grad_mine, grad, 1, 1, NARROW), shuffle, 1, 0, NARROW)
    right_gram = mm(mm(grad, pick, 1, 0, NARROW), grad, 0, 0, NARROW)
    return update, left_gram, right_gram


def local(partials, owner, left_stats, right_stats, left_root, right_root):
    n_y, n_z = lax.axis_size("y"), lax.axis_size("z")
    n_rep = lax.axis_size("x") * n_y * 2
    half = n_rep // 2
    core, plane = lax.axis_index("c"), lax.axis_index("z")
    my_xy = lax.axis_index("x") * n_y + lax.axis_index("y")
    _, _, n_rows, order = partials.shape
    out = routes(n_rep, n_z)
    home = [(b, a) for a, b in out]

    swapped = owner[1] < owner[0]
    roots = jnp.stack([left_root, right_root], axis=1)
    roots = jnp.where(swapped, roots[::-1], roots)
    roots = lax.ppermute(roots, EVERY, out)

    pieces = partials[0].reshape(n_rep, 2, n_rows, order)
    pieces = lax.all_to_all(pieces, REP, 0, 0, tiled=True)
    grad = jnp.sum(pieces.astype(WIDE), axis=0).astype(NARROW)

    slab = lax.ppermute(grad, EVERY, out)
    roots = jnp.broadcast_to(roots[None], (half, 2, 2, n_rows, order)).reshape(n_rep, 2, n_rows, order)
    roots = lax.all_to_all(roots, REP, 0, 0, tiled=True)
    slab, roots = lax.optimization_barrier((slab, roots))
    slab = jnp.broadcast_to(slab[None], (half, 2, n_rows, order)).reshape(n_rep, n_rows, order)
    slab = lax.all_to_all(slab, REP, 0, 0, tiled=True)
    results = block_rows(
        slab.reshape(order, order),
        roots[:, 0].reshape(order, order),
        roots[:, 1].reshape(order, order),
        my_xy, plane, half, n_rows,
    )

    results = jnp.stack(results, axis=0).reshape(3, 2, n_rows, order)
    keep = lax.dynamic_index_in_dim(results, core, 1, keepdims=False)
    send = lax.dynamic_index_in_dim(results, 1 - core, 1, keepdims=False)
    got = lax.ppermute(send, "c", [(0, 1), (1, 0)])
    both = jnp.stack([jnp.where(core == 0, keep, got), jnp.where(core == 0, got, keep)], axis=1)
    both = lax.ppermute(both, EVERY, home)
    update, left_gram, right_gram = both[0], both[1].astype(WIDE), both[2].astype(WIDE)
    scale = (1.0 - BETA) / order
    new_left = (BETA * left_stats.astype(WIDE) + scale * left_gram).astype(NARROW)
    new_right = (BETA * right_stats.astype(WIDE) + scale * right_gram).astype(NARROW)
    return update, new_left, new_right


def solution(mesh, grid=(4, 4, 2)):
    n_z = mesh.devices.shape[1]
    fine = Mesh(mesh.devices.reshape(*grid, n_z), EVERY)
    rows = P(REP, "z", None)
    return jax.shard_map(
        local,
        mesh=fine,
        in_specs=(P(REP, None, "z", None), P(REP), rows, rows, rows, rows),
        out_specs=(rows, rows, rows),
        check_vma=False,
    )
```

```python
import jax
import jax.numpy as jnp
from jax import lax
from jax.experimental import pallas as pl
from jax.experimental.pallas import tpu as pltpu
from jax.sharding import Mesh, PartitionSpec as P

BETA = 0.9
EPS = 1e-06
NARROW = jnp.bfloat16
WIDE = jnp.float32
REP = ("x", "y", "c")
EVERY = ("x", "y", "c", "z")


def routes(n_rep, n_z):
    half = n_rep // 2
    pairs = []
    for g in range(n_rep):
        for z in range(n_z):
            q = (g + z) % n_rep
            pairs.append((g * n_z + z, (q % half * 2 + q // half) * n_z + g))
    return pairs


def mm(a, b, left, right):
    return lax.dot_general(a, b, (((left,), (right,)), ((), ())), preferred_element_type=WIDE)


def block_kernel(where_ref, slabs_ref, keep_ref, send_ref, grad_ref, left_ref, right_ref, second_ref):
    n_slabs, _, n_rows, order = slabs_ref.shape
    half = n_slabs // 2
    my_xy, core, plane = where_ref[0], where_ref[1], where_ref[2]

    def first_row(device):
        slab = (device // 2 + half * (device % 2) + n_slabs - plane) % n_slabs
        return pl.multiple_of(slab * n_rows, n_rows)

    for device in range(n_slabs):
        rows = pl.ds(first_row(device), n_rows)
        grad_ref[rows, :] = slabs_ref[device, 0]
        left_ref[rows, :] = slabs_ref[device, 1]
        right_ref[rows, :] = slabs_ref[device, 2]
    grad = grad_ref[...]
    first = mm(left_ref[...], grad, 1, 0).astype(NARROW)
    second = mm(first, right_ref[...], 1, 0)
    second_ref[...] = second
    wide = grad.astype(WIDE)
    entries = order * order
    factor = jnp.sqrt(jnp.sum(wide * wide) / entries + EPS) / jnp.sqrt(jnp.sum(second * second) / entries + EPS)

    starts = [first_row(my_xy * 2 + core), first_row(my_xy * 2 + 1 - core)]
    mine = jnp.concatenate([grad_ref[pl.ds(start, n_rows), :] for start in starts], axis=0)
    row = lax.broadcasted_iota(jnp.int32, (2 * n_rows, order), 0)
    column = lax.broadcasted_iota(jnp.int32, (2 * n_rows, order), 1)
    pick = (column == jnp.where(row < n_rows, starts[0] + row, starts[1] + row - n_rows)).astype(NARROW)
    columns = mm(pick, grad, 1, 1).astype(NARROW)
    left_gram = mm(mine, grad, 1, 1).astype(NARROW)
    right_gram = mm(columns, grad, 1, 0).astype(NARROW)
    for number, out_ref in enumerate((keep_ref, send_ref)):
        out_ref[0] = (second_ref[pl.ds(starts[number], n_rows), :] * factor).astype(NARROW)
        out_ref[1] = left_gram[number * n_rows : (number + 1) * n_rows]
        out_ref[2] = right_gram[number * n_rows : (number + 1) * n_rows]


def block_rows(where, slabs):
    _, _, n_rows, order = slabs.shape
    out = jax.ShapeDtypeStruct((3, n_rows, order), NARROW)
    vmem = pl.BlockSpec(memory_space=pltpu.VMEM)
    return pl.pallas_call(
        block_kernel,
        out_shape=(out, out),
        in_specs=[pl.BlockSpec(memory_space=pltpu.SMEM), vmem],
        out_specs=(vmem, vmem),
        scratch_shapes=[pltpu.VMEM((order, order), NARROW)] * 3 + [pltpu.VMEM((order, order), WIDE)],
        compiler_params=pltpu.CompilerParams(vmem_limit_bytes=24 * 1024 * 1024),
        name="block_rows",
    )(where, slabs)


def local(partials, owner, left_stats, right_stats, left_root, right_root):
    n_y, n_z = lax.axis_size("y"), lax.axis_size("z")
    n_rep = lax.axis_size("x") * n_y * 2
    half = n_rep // 2
    core, plane = lax.axis_index("c"), lax.axis_index("z")
    my_xy = lax.axis_index("x") * n_y + lax.axis_index("y")
    _, _, n_rows, order = partials.shape
    out = routes(n_rep, n_z)
    home = [(b, a) for a, b in out]

    pieces = partials[0].reshape(n_rep, 2, n_rows, order)
    pieces = lax.all_to_all(pieces, REP, 0, 0, tiled=True)
    grad = jnp.sum(pieces.astype(WIDE), axis=0).astype(NARROW)

    swapped = owner[1] < owner[0]
    roots = jnp.stack([left_root, right_root], axis=1)
    roots = jnp.where(swapped, roots[::-1], roots)
    slab = jnp.concatenate([grad[:, None], roots], axis=1)
    slab = lax.ppermute(slab, EVERY, out)

    slabs = jnp.broadcast_to(slab[None], (half, 2, 3, n_rows, order)).reshape(n_rep, 3, n_rows, order)
    slabs = lax.all_to_all(slabs, REP, 0, 0, tiled=True)
    keep, send = block_rows(jnp.stack([my_xy, core, plane]).astype(jnp.int32), slabs)

    got = lax.ppermute(send, "c", [(0, 1), (1, 0)])
    both = jnp.stack([jnp.where(core == 0, keep, got), jnp.where(core == 0, got, keep)], axis=1)
    both = lax.ppermute(both, EVERY, home)
    update, left_gram, right_gram = both[0], both[1].astype(WIDE), both[2].astype(WIDE)
    scale = (1.0 - BETA) / order
    new_left = (BETA * left_stats.astype(WIDE) + scale * left_gram).astype(NARROW)
    new_right = (BETA * right_stats.astype(WIDE) + scale * right_gram).astype(NARROW)
    return update, new_left, new_right


def solution(mesh, grid=(4, 4, 2)):
    n_z = mesh.devices.shape[1]
    fine = Mesh(mesh.devices.reshape(*grid, n_z), EVERY)
    rows = P(REP, "z", None)
    return jax.shard_map(
        local,
        mesh=fine,
        in_specs=(P(REP, None, "z", None), P(REP), rows, rows, rows, rows),
        out_specs=(rows, rows, rows),
        check_vma=False,
    )
```

```python
import jax
import jax.numpy as jnp
from jax import lax
from jax.experimental import pallas as pl
from jax.experimental.pallas import tpu as pltpu
from jax.sharding import Mesh, PartitionSpec as P

BETA = 0.9
EPS = 1e-06
NARROW = jnp.bfloat16
WIDE = jnp.float32
REP = ("x", "y", "c")
EVERY = ("x", "y", "c", "z")


def routes(n_rep, n_z):
    half = n_rep // 2
    across, along, home = [], [], []
    for g in range(n_rep):
        for z in range(n_z):
            q = (g + z) % n_rep
            via = (q % half * 2 + q // half) * n_z
            across.append((g * n_z + z, via + z))
            along.append((via + z, via + g))
            home.append((via + g, g * n_z + z))
    return across, along, home


def mm(a, b, left, right):
    return lax.dot_general(a, b, (((left,), (right,)), ((), ())), preferred_element_type=WIDE)


def arrange_kernel(plane_ref, pieces_ref, out_ref, sems):
    n_rep = pieces_ref.shape[0]
    half = n_rep // 2
    copies = []
    for device in range(n_rep):
        group = (device // 2 + half * (device % 2) + n_rep - plane_ref[0]) % n_rep
        copies.append(pltpu.make_async_copy(pieces_ref.at[group], out_ref.at[device], sems.at[device]))
        copies[-1].start()
    for copy in copies:
        copy.wait()


def arrange(plane, pieces):
    return pl.pallas_call(
        arrange_kernel,
        out_shape=jax.ShapeDtypeStruct(pieces.shape, pieces.dtype),
        in_specs=[pl.BlockSpec(memory_space=pltpu.SMEM), pl.BlockSpec(memory_space=pl.ANY)],
        out_specs=pl.BlockSpec(memory_space=pltpu.VMEM),
        scratch_shapes=[pltpu.SemaphoreType.DMA((pieces.shape[0],))],
        name="arrange",
    )(plane[None], pieces)


def block_kernel(where_ref, slabs_ref, keep_ref, send_ref, grad_ref, left_ref, right_ref, second_ref):
    n_slabs, _, n_rows, order = slabs_ref.shape
    half = n_slabs // 2
    my_xy, core, plane = where_ref[0], where_ref[1], where_ref[2]

    def first_row(device):
        slab = (device // 2 + half * (device % 2) + n_slabs - plane) % n_slabs
        return pl.multiple_of(slab * n_rows, n_rows)

    for device in range(n_slabs):
        rows = pl.ds(first_row(device), n_rows)
        grad_ref[rows, :] = slabs_ref[device, 0]
        left_ref[rows, :] = slabs_ref[device, 1]
        right_ref[rows, :] = slabs_ref[device, 2]
    grad = grad_ref[...]
    first = mm(left_ref[...], grad, 1, 0).astype(NARROW)
    second = mm(first, right_ref[...], 1, 0)
    second_ref[...] = second
    wide = grad.astype(WIDE)
    entries = order * order
    factor = jnp.sqrt(jnp.sum(wide * wide) / entries + EPS) / jnp.sqrt(jnp.sum(second * second) / entries + EPS)

    starts = [first_row(my_xy * 2 + core), first_row(my_xy * 2 + 1 - core)]
    mine = jnp.concatenate([grad_ref[pl.ds(start, n_rows), :] for start in starts], axis=0)
    row = lax.broadcasted_iota(jnp.int32, (2 * n_rows, order), 0)
    column = lax.broadcasted_iota(jnp.int32, (2 * n_rows, order), 1)
    pick = (column == jnp.where(row < n_rows, starts[0] + row, starts[1] + row - n_rows)).astype(NARROW)
    columns = mm(pick, grad, 1, 1).astype(NARROW)
    left_gram = mm(mine, grad, 1, 1).astype(NARROW)
    right_gram = mm(columns, grad, 1, 0).astype(NARROW)
    for number, out_ref in enumerate((keep_ref, send_ref)):
        out_ref[0] = (second_ref[pl.ds(starts[number], n_rows), :] * factor).astype(NARROW)
        out_ref[1] = left_gram[number * n_rows : (number + 1) * n_rows]
        out_ref[2] = right_gram[number * n_rows : (number + 1) * n_rows]


def block_rows(where, slabs):
    _, _, n_rows, order = slabs.shape
    out = jax.ShapeDtypeStruct((3, n_rows, order), NARROW)
    vmem = pl.BlockSpec(memory_space=pltpu.VMEM)
    return pl.pallas_call(
        block_kernel,
        out_shape=(out, out),
        in_specs=[pl.BlockSpec(memory_space=pltpu.SMEM), vmem],
        out_specs=(vmem, vmem),
        scratch_shapes=[pltpu.VMEM((order, order), NARROW)] * 3 + [pltpu.VMEM((order, order), WIDE)],
        compiler_params=pltpu.CompilerParams(vmem_limit_bytes=24 * 1024 * 1024),
        name="block_rows",
    )(where, slabs)


def local(partials, owner, left_stats, right_stats, left_root, right_root):
    n_y, n_z = lax.axis_size("y"), lax.axis_size("z")
    n_rep = lax.axis_size("x") * n_y * 2
    half = n_rep // 2
    core, plane = lax.axis_index("c"), lax.axis_index("z")
    my_xy = lax.axis_index("x") * n_y + lax.axis_index("y")
    _, _, n_rows, order = partials.shape
    across, along, home = routes(n_rep, n_z)

    pieces = arrange(plane, partials[0].reshape(n_rep, 2, n_rows, order))
    pieces = lax.all_to_all(pieces, REP, 0, 0, tiled=True)
    grad = jnp.sum(pieces.astype(WIDE), axis=0).astype(NARROW)

    swapped = owner[1] < owner[0]
    roots = jnp.stack([left_root, right_root], axis=1)
    roots = jnp.where(swapped, roots[::-1], roots)
    roots = lax.ppermute(roots, EVERY, across)
    slab = jnp.concatenate([grad[:, None], roots], axis=1)
    slab = lax.ppermute(slab, EVERY, along)

    slabs = jnp.broadcast_to(slab[None], (half, 2, 3, n_rows, order)).reshape(n_rep, 3, n_rows, order)
    slabs = lax.all_to_all(slabs, REP, 0, 0, tiled=True)
    keep, send = block_rows(jnp.stack([my_xy, core, plane]).astype(jnp.int32), slabs)

    got = lax.ppermute(send, "c", [(0, 1), (1, 0)])
    both = jnp.stack([jnp.where(core == 0, keep, got), jnp.where(core == 0, got, keep)], axis=1)
    both = lax.ppermute(both, EVERY, home)
    update, left_gram, right_gram = both[0], both[1].astype(WIDE), both[2].astype(WIDE)
    scale = (1.0 - BETA) / order
    new_left = (BETA * left_stats.astype(WIDE) + scale * left_gram).astype(NARROW)
    new_right = (BETA * right_stats.astype(WIDE) + scale * right_gram).astype(NARROW)
    return update, new_left, new_right


def solution(mesh, grid=(4, 4, 2)):
    n_z = mesh.devices.shape[1]
    fine = Mesh(mesh.devices.reshape(*grid, n_z), EVERY)
    rows = P(REP, "z", None)
    return jax.shard_map(
        local,
        mesh=fine,
        in_specs=(P(REP, None, "z", None), P(REP), rows, rows, rows, rows),
        out_specs=(rows, rows, rows),
        check_vma=False,
    )
```

```python
import jax
import jax.numpy as jnp
from jax import lax
from jax.experimental import pallas as pl
from jax.experimental.pallas import tpu as pltpu
from jax.sharding import Mesh, PartitionSpec as P

BETA = 0.9
EPS = 1e-06
NARROW = jnp.bfloat16
WIDE = jnp.float32
REP = ("x", "y", "c")
EVERY = ("x", "y", "c", "z")


def routes(n_rep, n_z):
    half = n_rep // 2
    across, along, home, planes = [], [], [], [[] for _ in range(n_z)]
    for g in range(n_rep):
        for z in range(n_z):
            q = (g + z) % n_rep
            via = (q % half * 2 + q // half) * n_z
            across.append((g * n_z + z, via + z))
            along.append((via + z, via + g))
            home.append((via + g, g * n_z + z))
            planes[z].append(via + z)
    return across, along, home, planes


def mm(a, b, left, right):
    return lax.dot_general(a, b, (((left,), (right,)), ((), ())), preferred_element_type=WIDE)


def block_kernel(where_ref, slabs_ref, keep_ref, send_ref, grad_ref, left_ref, right_ref, second_ref):
    n_slabs, _, n_rows, order = slabs_ref.shape
    half = n_slabs // 2
    my_xy, core, plane = where_ref[0], where_ref[1], where_ref[2]

    def first_row(device):
        slab = (device // 2 + half * (device % 2) + n_slabs - plane) % n_slabs
        return pl.multiple_of(slab * n_rows, n_rows)

    for device in range(n_slabs):
        rows = pl.ds(first_row(device), n_rows)
        grad_ref[rows, :] = slabs_ref[device, 0]
        left_ref[rows, :] = slabs_ref[device, 1]
        right_ref[rows, :] = slabs_ref[device, 2]
    grad = grad_ref[...]
    first = mm(left_ref[...], grad, 1, 0).astype(NARROW)
    second = mm(first, right_ref[...], 1, 0)
    second_ref[...] = second
    wide = grad.astype(WIDE)
    entries = order * order
    factor = jnp.sqrt(jnp.sum(wide * wide) / entries + EPS) / jnp.sqrt(jnp.sum(second * second) / entries + EPS)

    starts = [first_row(my_xy * 2 + core), first_row(my_xy * 2 + 1 - core)]
    mine = jnp.concatenate([grad_ref[pl.ds(start, n_rows), :] for start in starts], axis=0)
    row = lax.broadcasted_iota(jnp.int32, (2 * n_rows, order), 0)
    column = lax.broadcasted_iota(jnp.int32, (2 * n_rows, order), 1)
    pick = (column == jnp.where(row < n_rows, starts[0] + row, starts[1] + row - n_rows)).astype(NARROW)
    columns = mm(pick, grad, 1, 1).astype(NARROW)
    left_gram = mm(mine, grad, 1, 1).astype(NARROW)
    right_gram = mm(columns, grad, 1, 0).astype(NARROW)
    for number, out_ref in enumerate((keep_ref, send_ref)):
        out_ref[0] = (second_ref[pl.ds(starts[number], n_rows), :] * factor).astype(NARROW)
        out_ref[1] = left_gram[number * n_rows : (number + 1) * n_rows]
        out_ref[2] = right_gram[number * n_rows : (number + 1) * n_rows]


def block_rows(where, slabs):
    _, _, n_rows, order = slabs.shape
    out = jax.ShapeDtypeStruct((3, n_rows, order), NARROW)
    vmem = pl.BlockSpec(memory_space=pltpu.VMEM)
    return pl.pallas_call(
        block_kernel,
        out_shape=(out, out),
        in_specs=[pl.BlockSpec(memory_space=pltpu.SMEM), vmem],
        out_specs=(vmem, vmem),
        scratch_shapes=[pltpu.VMEM((order, order), NARROW)] * 3 + [pltpu.VMEM((order, order), WIDE)],
        compiler_params=pltpu.CompilerParams(vmem_limit_bytes=24 * 1024 * 1024),
        name="block_rows",
    )(where, slabs)


def local(partials, owner, left_stats, right_stats, left_root, right_root):
    n_y, n_z = lax.axis_size("y"), lax.axis_size("z")
    n_rep = lax.axis_size("x") * n_y * 2
    half = n_rep // 2
    core, plane = lax.axis_index("c"), lax.axis_index("z")
    my_xy = lax.axis_index("x") * n_y + lax.axis_index("y")
    _, _, n_rows, order = partials.shape
    across, along, home, planes = routes(n_rep, n_z)

    pieces = partials[0].reshape(n_rep, 2, n_rows, order)
    pieces = lax.all_to_all(pieces, EVERY, 0, 0, axis_index_groups=planes, tiled=True)
    grad = jnp.sum(pieces.astype(WIDE), axis=0).astype(NARROW)

    swapped = owner[1] < owner[0]
    roots = jnp.stack([left_root, right_root], axis=1)
    roots = jnp.where(swapped, roots[::-1], roots)
    roots = lax.ppermute(roots, EVERY, across)
    roots = lax.ppermute(roots, EVERY, along)
    grad = lax.ppermute(grad, EVERY, along)
    slab = jnp.concatenate([grad[:, None], roots], axis=1)

    slabs = jnp.broadcast_to(slab[None], (half, 2, 3, n_rows, order)).reshape(n_rep, 3, n_rows, order)
    slabs = lax.all_to_all(slabs, REP, 0, 0, tiled=True)
    keep, send = block_rows(jnp.stack([my_xy, core, plane]).astype(jnp.int32), slabs)

    got = lax.ppermute(send, "c", [(0, 1), (1, 0)])
    both = jnp.stack([jnp.where(core == 0, keep, got), jnp.where(core == 0, got, keep)], axis=1)
    both = lax.ppermute(both, EVERY, home)
    update, left_gram, right_gram = both[0], both[1].astype(WIDE), both[2].astype(WIDE)
    scale = (1.0 - BETA) / order
    new_left = (BETA * left_stats.astype(WIDE) + scale * left_gram).astype(NARROW)
    new_right = (BETA * right_stats.astype(WIDE) + scale * right_gram).astype(NARROW)
    return update, new_left, new_right


def solution(mesh, grid=(4, 4, 2)):
    n_z = mesh.devices.shape[1]
    fine = Mesh(mesh.devices.reshape(*grid, n_z), EVERY)
    rows = P(REP, "z", None)
    return jax.shard_map(
        local,
        mesh=fine,
        in_specs=(P(REP, None, "z", None), P(REP), rows, rows, rows, rows),
        out_specs=(rows, rows, rows),
        check_vma=False,
    )
```

```python
import jax
import jax.numpy as jnp
from jax import lax
from jax.experimental import pallas as pl
from jax.experimental.pallas import tpu as pltpu
from jax.sharding import Mesh, PartitionSpec as P

BETA = 0.9
EPS = 1e-06
NARROW = jnp.bfloat16
WIDE = jnp.float32
REP = ("x", "y", "c")
EVERY = ("x", "y", "c", "z")


def routes(n_rep, n_z):
    half = n_rep // 2
    across, along, home, planes = [], [], [], [[] for _ in range(n_z)]
    for g in range(n_rep):
        for z in range(n_z):
            plane = g // 2 + half * (g % 2)
            q = (plane + z) % n_rep
            via = (q % half * 2 + q // half) * n_z
            across.append((g * n_z + z, via + z))
            along.append((via + z, via + plane))
            home.append((via + plane, g * n_z + z))
            planes[z].append(via + z)
    return across, along, home, planes


def mm(a, b, left, right):
    return lax.dot_general(a, b, (((left,), (right,)), ((), ())), preferred_element_type=WIDE)


def half_of(roots, plane, n_z):
    order = roots.shape[-1]
    tile = order // 4
    band = plane // (n_z // 4)
    twice = jnp.concatenate([roots, roots], axis=-1)
    near = lax.select_n(band, *[twice[..., k * tile : (k + 2) * tile] for k in range(4)])
    far = lax.select_n(band, *[twice[:, k // 2, :, (k + 2) * tile : (k + 3) * tile] for k in range(4)])
    return jnp.concatenate([near[:, 0], near[:, 1], far], axis=-1)


def block_kernel(where_ref, slabs_ref, keep_ref, send_ref, grad_ref, roots_ref, second_ref):
    n_slabs, n_rows, _ = slabs_ref.shape
    order = grad_ref.shape[0]
    tile = order // 4
    half = n_slabs // 2
    my_xy, core, plane = where_ref[0], where_ref[1], where_ref[2]

    def slab_of(device):
        return (device // 2 + half * (device % 2) + n_slabs - plane) % n_slabs

    def first_row(device):
        return pl.multiple_of(slab_of(device) * n_rows, n_rows)

    roots_ref[...] = jnp.zeros_like(roots_ref)
    for device in range(n_slabs):
        rows = pl.ds(first_row(device), n_rows)
        band = slab_of(device) // (n_slabs // 4)
        columns = [pl.ds(pl.multiple_of((band + k) % 4 * tile, tile), tile) for k in range(3)]
        grad_ref[rows, :] = slabs_ref[device, :, :order]
        for number, (side, k) in enumerate(((0, 0), (0, 1), (1, 0), (1, 1), (band // 2, 2))):
            start = order + number * tile
            roots_ref[side, rows, columns[k]] = slabs_ref[device, :, start : start + tile]
    grad = grad_ref[...]
    left, right = roots_ref[0], roots_ref[1]
    diagonal = lax.broadcasted_iota(jnp.int32, (order, order), 0) // tile == (
        lax.broadcasted_iota(jnp.int32, (order, order), 1) // tile
    )
    zero = jnp.zeros((), NARROW)
    first = (mm(left, grad, 1, 0) + mm(jnp.where(diagonal, zero, left), grad, 0, 0)).astype(NARROW)
    second = mm(first, right, 1, 0) + mm(first, jnp.where(diagonal, zero, right), 1, 1)
    second_ref[...] = second
    wide = grad.astype(WIDE)
    entries = order * order
    factor = jnp.sqrt(jnp.sum(wide * wide) / entries + EPS) / jnp.sqrt(jnp.sum(second * second) / entries + EPS)

    starts = [first_row(my_xy * 2 + core), first_row(my_xy * 2 + 1 - core)]
    mine = jnp.concatenate([grad_ref[pl.ds(start, n_rows), :] for start in starts], axis=0)
    row = lax.broadcasted_iota(jnp.int32, (2 * n_rows, order), 0)
    column = lax.broadcasted_iota(jnp.int32, (2 * n_rows, order), 1)
    pick = (column == jnp.where(row < n_rows, starts[0] + row, starts[1] + row - n_rows)).astype(NARROW)
    columns = mm(pick, grad, 1, 1).astype(NARROW)
    left_gram = mm(mine, grad, 1, 1).astype(NARROW)
    right_gram = mm(columns, grad, 1, 0).astype(NARROW)
    for number, out_ref in enumerate((keep_ref, send_ref)):
        out_ref[0] = (second_ref[pl.ds(starts[number], n_rows), :] * factor).astype(NARROW)
        out_ref[1] = left_gram[number * n_rows : (number + 1) * n_rows]
        out_ref[2] = right_gram[number * n_rows : (number + 1) * n_rows]


def block_rows(where, slabs, order):
    n_rows = slabs.shape[1]
    out = jax.ShapeDtypeStruct((3, n_rows, order), NARROW)
    vmem = pl.BlockSpec(memory_space=pltpu.VMEM)
    return pl.pallas_call(
        block_kernel,
        out_shape=(out, out),
        in_specs=[pl.BlockSpec(memory_space=pltpu.SMEM), vmem],
        out_specs=(vmem, vmem),
        scratch_shapes=[
            pltpu.VMEM((order, order), NARROW),
            pltpu.VMEM((2, order, order), NARROW),
            pltpu.VMEM((order, order), WIDE),
        ],
        compiler_params=pltpu.CompilerParams(vmem_limit_bytes=24 * 1024 * 1024),
        name="block_rows",
    )(where, slabs)


def local(partials, owner, left_stats, right_stats, left_root, right_root):
    n_y, n_z = lax.axis_size("y"), lax.axis_size("z")
    n_rep = lax.axis_size("x") * n_y * 2
    half = n_rep // 2
    core, plane = lax.axis_index("c"), lax.axis_index("z")
    my_xy = lax.axis_index("x") * n_y + lax.axis_index("y")
    _, _, n_rows, order = partials.shape
    across, along, home, planes = routes(n_rep, n_z)

    pieces = partials[0].reshape(n_rep, 2, n_rows, order)
    pieces = lax.all_to_all(pieces, EVERY, 0, 0, axis_index_groups=planes, tiled=True)
    grad = jnp.sum(pieces.astype(WIDE), axis=0).astype(NARROW)

    swapped = owner[1] < owner[0]
    roots = jnp.stack([left_root, right_root], axis=1)
    roots = jnp.where(swapped, roots[::-1], roots)
    roots = lax.ppermute(half_of(roots, plane, n_z), EVERY, across)
    slab = jnp.concatenate([grad, roots], axis=-1)
    slab = lax.ppermute(slab, EVERY, along)

    slabs = jnp.broadcast_to(slab[None], (half, *slab.shape)).reshape(n_rep, n_rows, slab.shape[-1])
    slabs = lax.all_to_all(slabs, REP, 0, 0, tiled=True)
    keep, send = block_rows(jnp.stack([my_xy, core, plane]).astype(jnp.int32), slabs, order)

    got = lax.ppermute(send, "c", [(0, 1), (1, 0)])
    both = jnp.stack([jnp.where(core == 0, keep, got), jnp.where(core == 0, got, keep)], axis=1)
    both = lax.ppermute(both, EVERY, home)
    update, left_gram, right_gram = both[0], both[1].astype(WIDE), both[2].astype(WIDE)
    scale = (1.0 - BETA) / order
    new_left = (BETA * left_stats.astype(WIDE) + scale * left_gram).astype(NARROW)
    new_right = (BETA * right_stats.astype(WIDE) + scale * right_gram).astype(NARROW)
    return update, new_left, new_right


def solution(mesh, grid=(4, 4, 2)):
    n_z = mesh.devices.shape[1]
    fine = Mesh(mesh.devices.reshape(*grid, n_z), EVERY)
    rows = P(REP, "z", None)
    return jax.shard_map(
        local,
        mesh=fine,
        in_specs=(P(REP, None, "z", None), P(REP), rows, rows, rows, rows),
        out_specs=(rows, rows, rows),
        check_vma=False,
    )
```

```python
import jax
import jax.numpy as jnp
from jax import lax
from jax.experimental import pallas as pl
from jax.experimental.pallas import tpu as pltpu
from jax.sharding import Mesh, PartitionSpec as P

BETA = 0.9
EPS = 1e-06
NARROW = jnp.bfloat16
WIDE = jnp.float32
REP = ("x", "y", "c")
EVERY = ("x", "y", "c", "z")


def turned(xy, half):
    return {0: half // 2, half // 2: 0}.get(xy, xy)


def index_of(device, half):
    return turned(device // 2, half) + half * (1 - device % 2)


def routes(n_rep, n_z):
    half = n_rep // 2
    across, along, home, planes = [], [], [], [[] for _ in range(n_z)]
    for g in range(n_rep):
        for z in range(n_z):
            plane = g // 2 + half * (1 - g % 2)
            q = (plane + z) % n_rep
            via = (turned(q % half, half) * 2 + 1 - q // half) * n_z
            across.append((g * n_z + z, via + z))
            along.append((via + z, via + plane))
            home.append((via + plane, g * n_z + z))
            planes[z].append(via + z)
    return across, along, home, planes


def mm(a, b, left, right):
    return lax.dot_general(a, b, (((left,), (right,)), ((), ())), preferred_element_type=WIDE)


def half_of(roots, plane, n_z):
    order = roots.shape[-1]
    tile = order // 4
    band = plane // (n_z // 4)
    twice = jnp.concatenate([roots, roots], axis=-1)
    near = lax.select_n(band, *[twice[..., k * tile : (k + 2) * tile] for k in range(4)])
    far = lax.select_n(band, *[twice[:, k // 2, :, (k + 2) * tile : (k + 3) * tile] for k in range(4)])
    return jnp.concatenate([near[:, 0], near[:, 1], far], axis=-1)


def block_kernel(where_ref, slabs_ref, keep_ref, send_ref, grad_ref, roots_ref, second_ref):
    n_slabs, n_rows, _ = slabs_ref.shape
    order = grad_ref.shape[0]
    tile = order // 4
    half = n_slabs // 2
    plane, slabs_here = where_ref[0], (where_ref[1], where_ref[2])

    def slab_of(device):
        return (index_of(device, half) + n_slabs - plane) % n_slabs

    def first_row(slab):
        return pl.multiple_of(slab * n_rows, n_rows)

    for device in range(n_slabs):
        rows = pl.ds(first_row(slab_of(device)), n_rows)
        band = slab_of(device) // (n_slabs // 4)
        columns = [pl.ds(pl.multiple_of((band + k) % 4 * tile, tile), tile) for k in range(3)]
        grad_ref[rows, :] = slabs_ref[device, :, :order]
        for number, (side, k) in enumerate(((0, 0), (0, 1), (1, 0), (1, 1), (band // 2, 2))):
            start = order + number * tile
            roots_ref[side, rows, columns[k]] = slabs_ref[device, :, start : start + tile]
    for band in range(4):
        for side, k in ((0, 1), (1, 1), (band // 2, 2)):
            across = (band + k) % 4 * tile
            there, here = pl.ds(across, tile), pl.ds(band * tile, tile)
            roots_ref[side, there, here] = roots_ref[side, here, there].T
    grad = grad_ref[...]
    first = mm(roots_ref[0], grad, 1, 0).astype(NARROW)
    second = mm(first, roots_ref[1], 1, 0)
    second_ref[...] = second
    wide = grad.astype(WIDE)
    entries = order * order
    factor = jnp.sqrt(jnp.sum(wide * wide) / entries + EPS) / jnp.sqrt(jnp.sum(second * second) / entries + EPS)

    starts = [first_row(slab) for slab in slabs_here]
    mine = jnp.concatenate([grad_ref[pl.ds(start, n_rows), :] for start in starts], axis=0)
    row = lax.broadcasted_iota(jnp.int32, (2 * n_rows, order), 0)
    column = lax.broadcasted_iota(jnp.int32, (2 * n_rows, order), 1)
    pick = (column == jnp.where(row < n_rows, starts[0] + row, starts[1] + row - n_rows)).astype(NARROW)
    columns = mm(pick, grad, 1, 1).astype(NARROW)
    left_gram = mm(mine, grad, 1, 1).astype(NARROW)
    right_gram = mm(columns, grad, 1, 0).astype(NARROW)
    for number, out_ref in enumerate((keep_ref, send_ref)):
        out_ref[0] = (second_ref[pl.ds(starts[number], n_rows), :] * factor).astype(NARROW)
        out_ref[1] = left_gram[number * n_rows : (number + 1) * n_rows]
        out_ref[2] = right_gram[number * n_rows : (number + 1) * n_rows]


def block_rows(where, slabs, order):
    n_rows = slabs.shape[1]
    out = jax.ShapeDtypeStruct((3, n_rows, order), NARROW)
    vmem = pl.BlockSpec(memory_space=pltpu.VMEM)
    return pl.pallas_call(
        block_kernel,
        out_shape=(out, out),
        in_specs=[pl.BlockSpec(memory_space=pltpu.SMEM), vmem],
        out_specs=(vmem, vmem),
        scratch_shapes=[
            pltpu.VMEM((order, order), NARROW),
            pltpu.VMEM((2, order, order), NARROW),
            pltpu.VMEM((order, order), WIDE),
        ],
        compiler_params=pltpu.CompilerParams(vmem_limit_bytes=24 * 1024 * 1024),
        name="block_rows",
    )(where, slabs)


def local(partials, owner, left_stats, right_stats, left_root, right_root):
    n_y, n_z = lax.axis_size("y"), lax.axis_size("z")
    n_rep = lax.axis_size("x") * n_y * 2
    half = n_rep // 2
    core, plane = lax.axis_index("c"), lax.axis_index("z")
    my_xy = lax.axis_index("x") * n_y + lax.axis_index("y")
    _, _, n_rows, order = partials.shape
    across, along, home, planes = routes(n_rep, n_z)

    pieces = partials[0].reshape(n_rep, 2, n_rows, order)
    pieces = lax.all_to_all(pieces, EVERY, 0, 0, axis_index_groups=planes, tiled=True)
    grad = jnp.sum(pieces.astype(WIDE), axis=0).astype(NARROW)

    swapped = owner[1] < owner[0]
    roots = jnp.stack([left_root, right_root], axis=1)
    roots = jnp.where(swapped, roots[::-1], roots)
    roots = lax.ppermute(half_of(roots, plane, n_z), EVERY, across)
    slab = jnp.concatenate([grad, roots], axis=-1)
    slab = lax.ppermute(slab, EVERY, along)

    slabs = jnp.broadcast_to(slab[None], (half, *slab.shape)).reshape(n_rep, n_rows, slab.shape[-1])
    slabs = lax.all_to_all(slabs, REP, 0, 0, tiled=True)
    index = jnp.array([index_of(2 * xy, half) for xy in range(half)], jnp.int32)[my_xy]
    here = [(index + half * core + n_z - plane) % n_rep, (index + half * (1 - core) + n_z - plane) % n_rep]
    keep, send = block_rows(jnp.stack([plane, *here]).astype(jnp.int32), slabs, order)

    got = lax.ppermute(send, "c", [(0, 1), (1, 0)])
    both = jnp.stack([jnp.where(core == 0, keep, got), jnp.where(core == 0, got, keep)], axis=1)
    both = lax.ppermute(both, EVERY, home)
    update, left_gram, right_gram = both[0], both[1].astype(WIDE), both[2].astype(WIDE)
    scale = (1.0 - BETA) / order
    new_left = (BETA * left_stats.astype(WIDE) + scale * left_gram).astype(NARROW)
    new_right = (BETA * right_stats.astype(WIDE) + scale * right_gram).astype(NARROW)
    return update, new_left, new_right


def solution(mesh, grid=(4, 4, 2)):
    n_z = mesh.devices.shape[1]
    fine = Mesh(mesh.devices.reshape(*grid, n_z), EVERY)
    rows = P(REP, "z", None)
    return jax.shard_map(
        local,
        mesh=fine,
        in_specs=(P(REP, None, "z", None), P(REP), rows, rows, rows, rows),
        out_specs=(rows, rows, rows),
        check_vma=False,
    )
```

```python
import jax
import jax.numpy as jnp
from jax import lax
from jax.experimental import pallas as pl
from jax.experimental.pallas import tpu as pltpu
from jax.sharding import Mesh, PartitionSpec as P

BETA = 0.9
EPS = 1e-06
NARROW = jnp.bfloat16
WIDE = jnp.float32
REP = ("x", "y", "c")
EVERY = ("x", "y", "c", "z")


def turned(xy, half):
    return {0: half // 2, half // 2: 0}.get(xy, xy)


def index_of(device, half):
    return turned(device // 2, half) + half * (1 - device % 2)


def routes(n_rep, n_z):
    half = n_rep // 2
    across, along, home, planes = [], [], [], [[] for _ in range(n_z)]
    for g in range(n_rep):
        for z in range(n_z):
            plane = g // 2 + half * (1 - g % 2)
            q = (plane + z) % n_rep
            via = (turned(q % half, half) * 2 + 1 - q // half) * n_z
            across.append((g * n_z + z, via + z))
            along.append((via + z, via + plane))
            home.append((via + plane, g * n_z + z))
            planes[z].append(via + z)
    return across, along, home, planes


def mm(a, b, left, right):
    return lax.dot_general(a, b, (((left,), (right,)), ((), ())), preferred_element_type=WIDE)


def half_of(roots, plane, n_z):
    order = roots.shape[-1]
    tile = order // 4
    band = plane // (n_z // 4)
    twice = jnp.concatenate([roots, roots], axis=-1)
    near = lax.select_n(band, *[twice[..., k * tile : (k + 2) * tile] for k in range(4)])
    far = lax.select_n(band, *[twice[:, k // 2, :, (k + 2) * tile : (k + 3) * tile] for k in range(4)])
    return jnp.concatenate([near[:, 0], near[:, 1], far], axis=-1)


def block_kernel(where_ref, grads_ref, halves_ref, keep_ref, send_ref, grad_ref, roots_ref, second_ref):
    n_slabs, n_rows, _ = grads_ref.shape
    order = grad_ref.shape[0]
    tile = order // 4
    half = n_slabs // 2
    plane, slabs_here = where_ref[0], (where_ref[1], where_ref[2])

    def slab_of(device):
        return (index_of(device, half) + n_slabs - plane) % n_slabs

    def first_row(slab):
        return pl.multiple_of(slab * n_rows, n_rows)

    for device in range(n_slabs):
        rows = pl.ds(first_row(slab_of(device)), n_rows)
        band = slab_of(device) // (n_slabs // 4)
        columns = [pl.ds(pl.multiple_of((band + k) % 4 * tile, tile), tile) for k in range(3)]
        grad_ref[rows, :] = grads_ref[device]
        for number, (side, k) in enumerate(((0, 0), (0, 1), (1, 0), (1, 1), (band // 2, 2))):
            start = number * tile
            roots_ref[side, rows, columns[k]] = halves_ref[device, :, start : start + tile]
    for band in range(4):
        for side, k in ((0, 1), (1, 1), (band // 2, 2)):
            across = (band + k) % 4 * tile
            there, here = pl.ds(across, tile), pl.ds(band * tile, tile)
            roots_ref[side, there, here] = roots_ref[side, here, there].T
    grad = grad_ref[...]
    first = mm(roots_ref[0], grad, 1, 0).astype(NARROW)
    second = mm(first, roots_ref[1], 1, 0)
    second_ref[...] = second
    wide = grad.astype(WIDE)
    entries = order * order
    factor = jnp.sqrt(jnp.sum(wide * wide) / entries + EPS) / jnp.sqrt(jnp.sum(second * second) / entries + EPS)

    starts = [first_row(slab) for slab in slabs_here]
    mine = jnp.concatenate([grad_ref[pl.ds(start, n_rows), :] for start in starts], axis=0)
    row = lax.broadcasted_iota(jnp.int32, (2 * n_rows, order), 0)
    column = lax.broadcasted_iota(jnp.int32, (2 * n_rows, order), 1)
    pick = (column == jnp.where(row < n_rows, starts[0] + row, starts[1] + row - n_rows)).astype(NARROW)
    columns = mm(pick, grad, 1, 1).astype(NARROW)
    left_gram = mm(mine, grad, 1, 1).astype(NARROW)
    right_gram = mm(columns, grad, 1, 0).astype(NARROW)
    for number, out_ref in enumerate((keep_ref, send_ref)):
        out_ref[0] = (second_ref[pl.ds(starts[number], n_rows), :] * factor).astype(NARROW)
        out_ref[1] = left_gram[number * n_rows : (number + 1) * n_rows]
        out_ref[2] = right_gram[number * n_rows : (number + 1) * n_rows]


def block_rows(where, grads, halves):
    _, n_rows, order = grads.shape
    out = jax.ShapeDtypeStruct((3, n_rows, order), NARROW)
    vmem = pl.BlockSpec(memory_space=pltpu.VMEM)
    return pl.pallas_call(
        block_kernel,
        out_shape=(out, out),
        in_specs=[pl.BlockSpec(memory_space=pltpu.SMEM), vmem, vmem],
        out_specs=(vmem, vmem),
        scratch_shapes=[
            pltpu.VMEM((order, order), NARROW),
            pltpu.VMEM((2, order, order), NARROW),
            pltpu.VMEM((order, order), WIDE),
        ],
        compiler_params=pltpu.CompilerParams(vmem_limit_bytes=24 * 1024 * 1024),
        name="block_rows",
    )(where, grads, halves)


def local(partials, owner, left_stats, right_stats, left_root, right_root):
    n_y, n_z = lax.axis_size("y"), lax.axis_size("z")
    n_rep = lax.axis_size("x") * n_y * 2
    half = n_rep // 2
    core, plane = lax.axis_index("c"), lax.axis_index("z")
    my_xy = lax.axis_index("x") * n_y + lax.axis_index("y")
    _, _, n_rows, order = partials.shape
    across, along, home, planes = routes(n_rep, n_z)

    pieces = partials[0].reshape(n_rep, 2, n_rows, order)
    pieces = lax.all_to_all(pieces, EVERY, 0, 0, axis_index_groups=planes, tiled=True)
    grad = jnp.sum(pieces.astype(WIDE), axis=0).astype(NARROW)

    swapped = owner[1] < owner[0]
    roots = jnp.stack([left_root, right_root], axis=1)
    roots = jnp.where(swapped, roots[::-1], roots)
    roots = lax.ppermute(half_of(roots, plane, n_z), EVERY, across)
    slab = jnp.concatenate([grad, roots], axis=-1)
    slab = lax.ppermute(slab, EVERY, along)

    slabs = []
    for part in (slab[..., :order], slab[..., order:]):
        copies = jnp.broadcast_to(part[None], (half, *part.shape)).reshape(n_rep, n_rows, part.shape[-1])
        slabs.append(lax.all_to_all(copies, REP, 0, 0, tiled=True))
    index = jnp.array([index_of(2 * xy, half) for xy in range(half)], jnp.int32)[my_xy]
    here = [(index + half * core + n_z - plane) % n_rep, (index + half * (1 - core) + n_z - plane) % n_rep]
    keep, send = block_rows(jnp.stack([plane, *here]).astype(jnp.int32), *slabs)

    got = lax.ppermute(send, "c", [(0, 1), (1, 0)])
    both = jnp.stack([jnp.where(core == 0, keep, got), jnp.where(core == 0, got, keep)], axis=1)
    both = lax.ppermute(both, EVERY, home)
    update, left_gram, right_gram = both[0], both[1].astype(WIDE), both[2].astype(WIDE)
    scale = (1.0 - BETA) / order
    new_left = (BETA * left_stats.astype(WIDE) + scale * left_gram).astype(NARROW)
    new_right = (BETA * right_stats.astype(WIDE) + scale * right_gram).astype(NARROW)
    return update, new_left, new_right


def solution(mesh, grid=(4, 4, 2)):
    n_z = mesh.devices.shape[1]
    fine = Mesh(mesh.devices.reshape(*grid, n_z), EVERY)
    rows = P(REP, "z", None)
    return jax.shard_map(
        local,
        mesh=fine,
        in_specs=(P(REP, None, "z", None), P(REP), rows, rows, rows, rows),
        out_specs=(rows, rows, rows),
        check_vma=False,
    )
```

```python
import jax
import jax.numpy as jnp
from jax import lax
from jax.experimental import pallas as pl
from jax.experimental.pallas import tpu as pltpu
from jax.sharding import Mesh, PartitionSpec as P

BETA = 0.9
EPS = 1e-06
NARROW = jnp.bfloat16
WIDE = jnp.float32
REP = ("x", "y", "c")
EVERY = ("x", "y", "c", "z")


def turned(xy, half):
    return {0: half // 2, half // 2: 0}.get(xy, xy)


def index_of(device, half):
    return turned(device // 2, half) + half * (1 - device % 2)


def routes(n_rep, n_z):
    half = n_rep // 2
    across, along, home, planes = [], [], [], [[] for _ in range(n_z)]
    for g in range(n_rep):
        for z in range(n_z):
            plane = g // 2 + half * (1 - g % 2)
            q = (plane + z) % n_rep
            via = (turned(q % half, half) * 2 + 1 - q // half) * n_z
            across.append((g * n_z + z, via + z))
            along.append((via + z, via + plane))
            home.append((via + plane, g * n_z + z))
            planes[z].append(via + z)
    return across, along, home, planes


def mm(a, b, left, right):
    return lax.dot_general(a, b, (((left,), (right,)), ((), ())), preferred_element_type=WIDE)


def half_of(roots, plane, n_z):
    order = roots.shape[-1]
    tile = order // 4
    band = plane // (n_z // 4)
    twice = jnp.concatenate([roots, roots], axis=-1)
    near = lax.select_n(band, *[twice[..., k * tile : (k + 2) * tile] for k in range(4)])
    far = lax.select_n(band, *[twice[:, k // 2, :, (k + 2) * tile : (k + 3) * tile] for k in range(4)])
    return jnp.concatenate([near[:, 0], near[:, 1], far], axis=-1)


def block_kernel(where_ref, slabs_ref, keep_ref, send_ref, grad_ref, roots_ref, second_ref):
    n_slabs, n_rows, _ = slabs_ref.shape
    order = grad_ref.shape[0]
    tile = order // 4
    half = n_slabs // 2
    plane, slabs_here = where_ref[0], (where_ref[1], where_ref[2])

    def slab_of(device):
        return (index_of(device, half) + n_slabs - plane) % n_slabs

    def first_row(slab):
        return pl.multiple_of(slab * n_rows, n_rows)

    for device in range(n_slabs):
        rows = pl.ds(first_row(slab_of(device)), n_rows)
        band = slab_of(device) // (n_slabs // 4)
        columns = [pl.ds(pl.multiple_of((band + k) % 4 * tile, tile), tile) for k in range(3)]
        grad_ref[rows, :] = slabs_ref[device, :, :order]
        for number, (side, k) in enumerate(((0, 0), (0, 1), (1, 0), (1, 1), (band // 2, 2))):
            start = order + number * tile
            roots_ref[side, rows, columns[k]] = slabs_ref[device, :, start : start + tile]
    for band in range(4):
        for side, k in ((0, 1), (1, 1), (band // 2, 2)):
            across = (band + k) % 4 * tile
            there, here = pl.ds(across, tile), pl.ds(band * tile, tile)
            roots_ref[side, there, here] = roots_ref[side, here, there].T
    grad = grad_ref[...]
    first = mm(roots_ref[0], grad, 1, 0).astype(NARROW)
    second = mm(first, roots_ref[1], 1, 0)
    second_ref[...] = second
    wide = grad.astype(WIDE)
    entries = order * order
    factor = jnp.sqrt(jnp.sum(wide * wide) / entries + EPS) / jnp.sqrt(jnp.sum(second * second) / entries + EPS)

    starts = [first_row(slab) for slab in slabs_here]
    mine = jnp.concatenate([grad_ref[pl.ds(start, n_rows), :] for start in starts], axis=0)
    row = lax.broadcasted_iota(jnp.int32, (2 * n_rows, order), 0)
    column = lax.broadcasted_iota(jnp.int32, (2 * n_rows, order), 1)
    pick = (column == jnp.where(row < n_rows, starts[0] + row, starts[1] + row - n_rows)).astype(NARROW)
    columns = mm(pick, grad, 1, 1).astype(NARROW)
    left_gram = mm(mine, grad, 1, 1).astype(NARROW)
    right_gram = mm(columns, grad, 1, 0).astype(NARROW)
    for number, out_ref in enumerate((keep_ref, send_ref)):
        out_ref[0] = (second_ref[pl.ds(starts[number], n_rows), :] * factor).astype(NARROW)
        out_ref[1] = left_gram[number * n_rows : (number + 1) * n_rows]
        out_ref[2] = right_gram[number * n_rows : (number + 1) * n_rows]


def block_rows(where, slabs, order):
    n_rows = slabs.shape[1]
    out = jax.ShapeDtypeStruct((3, n_rows, order), NARROW)
    vmem = pl.BlockSpec(memory_space=pltpu.VMEM)
    return pl.pallas_call(
        block_kernel,
        out_shape=(out, out),
        in_specs=[pl.BlockSpec(memory_space=pltpu.SMEM), vmem],
        out_specs=(vmem, vmem),
        scratch_shapes=[
            pltpu.VMEM((order, order), NARROW),
            pltpu.VMEM((2, order, order), NARROW),
            pltpu.VMEM((order, order), WIDE),
        ],
        compiler_params=pltpu.CompilerParams(vmem_limit_bytes=24 * 1024 * 1024),
        name="block_rows",
    )(where, slabs)


def local(partials, owner, left_stats, right_stats, left_root, right_root):
    n_y, n_z = lax.axis_size("y"), lax.axis_size("z")
    n_rep = lax.axis_size("x") * n_y * 2
    half = n_rep // 2
    core, plane = lax.axis_index("c"), lax.axis_index("z")
    my_xy = lax.axis_index("x") * n_y + lax.axis_index("y")
    _, _, n_rows, order = partials.shape
    across, along, home, planes = routes(n_rep, n_z)

    pieces = partials[0].reshape(n_rep, 2, n_rows, order)
    pieces = lax.all_to_all(pieces, EVERY, 0, 0, axis_index_groups=planes, tiled=True)
    grad = jnp.sum(pieces.astype(WIDE), axis=0).astype(NARROW)

    swapped = owner[1] < owner[0]
    roots = jnp.stack([left_root, right_root], axis=1)
    roots = jnp.where(swapped, roots[::-1], roots)
    roots = lax.ppermute(half_of(roots, plane, n_z), EVERY, across)
    slab = jnp.concatenate([grad, roots], axis=-1)
    slab = lax.ppermute(slab, EVERY, along)

    slabs = jnp.broadcast_to(slab[None], (half, *slab.shape)).reshape(n_rep, n_rows, slab.shape[-1])
    slabs = lax.all_to_all(slabs, REP, 0, 0, tiled=True)
    index = half + jnp.where(my_xy == 0, half // 2, jnp.where(my_xy == half // 2, 0, my_xy))
    here = [(index + half * core + n_z - plane) % n_rep, (index + half * (1 - core) + n_z - plane) % n_rep]
    keep, send = block_rows(jnp.stack([plane, *here]).astype(jnp.int32), slabs, order)

    got = lax.ppermute(send, "c", [(0, 1), (1, 0)])
    both = jnp.stack([jnp.where(core == 0, keep, got), jnp.where(core == 0, got, keep)], axis=1)
    both = lax.ppermute(both, EVERY, home)
    update, left_gram, right_gram = both[0], both[1].astype(WIDE), both[2].astype(WIDE)
    scale = (1.0 - BETA) / order
    new_left = (BETA * left_stats.astype(WIDE) + scale * left_gram).astype(NARROW)
    new_right = (BETA * right_stats.astype(WIDE) + scale * right_gram).astype(NARROW)
    return update, new_left, new_right


def solution(mesh, grid=(4, 4, 2)):
    n_z = mesh.devices.shape[1]
    fine = Mesh(mesh.devices.reshape(*grid, n_z), EVERY)
    rows = P(REP, "z", None)
    return jax.shard_map(
        local,
        mesh=fine,
        in_specs=(P(REP, None, "z", None), P(REP), rows, rows, rows, rows),
        out_specs=(rows, rows, rows),
        check_vma=False,
    )
```
